512 devices in a mesh: seq: 128 (over z, x, core), mp: 4 (over y).
Axes of the slice: x: 4, y: 4, z: 16, core: 2. Of those that a mesh axis runs over, the one named last changes fastest.
Arguments:
- queries: bfloat16 [16384, 4096], P('seq', 'mp'), may hold values from -6 to 6
- keys: bfloat16 [16384, 4096], P('seq', 'mp'), may hold values from -6 to 6
- values: bfloat16 [16384, 4096], P('seq', 'mp'), may hold values from -6 to 6
- log_decay: float32 [16384, 32], P('seq', 'mp'), may hold values from -0.7 to 0, as said below
- norm_gain: float32 [4096], P('mp'), may hold values from 0.1 to 1.9
Outputs:
- attended: bfloat16 [16384, 4096], P(('seq', 'mp'))
The draws below stay inside these ranges and needn't reach their ends.
Inputs may be any that keep to these rules, and one draw needn't show every extreme that they name: `log_decay`: each entry is the logarithm of a decay factor in (0, 1].
All inputs are finite; a program needn't handle non-finite values.
Results may differ from the reference program's by a relative error of at most 0.0056.
Values may be sent and summed in bfloat16 or wider, within the bound.
No kernel may reach another device: no remote copies, remote signals or barrier semaphores. Data moves between devices by JAX's collectives and lax.ppermute only.
A program may use at most 192 MiB of HBM per device.

```python
import math
import jax
import jax.numpy as jnp
from jax import lax

HEAD_COUNT = 32
HEAD_DIM = 128
TOK_DEV = 128
WIDTH = 4096
TOKEN_COUNT = 16384


def stretch_tokens(key):
    blocks = TOKEN_COUNT // TOK_DEV
    span = min(max(6, blocks // 8), blocks - 1)
    first = jax.random.randint(jax.random.fold_in(key, 101), (), 1, blocks - span + 1)
    block_of = jnp.arange(TOKEN_COUNT) // TOK_DEV
    return (block_of >= first) & (block_of < first + span)


def split_rows(key, inside, upper_side):
    entries = jnp.clip(jax.random.normal(key, (TOKEN_COUNT, HEAD_COUNT, HEAD_DIM), jnp.float32), -6.0, 6.0)
    upper = jnp.arange(HEAD_DIM) >= HEAD_DIM // 2
    if upper_side:
        silent = upper
    else:
        silent = jnp.logical_not(upper)
    blanked = inside[:, None, None] & silent[None, None, :]
    return jnp.where(blanked, 0.0, entries).reshape(TOKEN_COUNT, WIDTH).astype(jnp.float32)


def draw_queries(key, part):
    inside = stretch_tokens(key)
    key = jax.random.fold_in(key, 7)
    return split_rows(key, inside, True).astype(jnp.bfloat16)


def draw_keys(key, part):
    inside = stretch_tokens(key)
    key = jax.random.fold_in(key, 9)
    return split_rows(key, inside, False).astype(jnp.bfloat16)


def draw_log_decay(key, part):
    key = jax.random.fold_in(key, 3)
    pieces = jax.random.split(key, 7)
    fast_count = 3 * HEAD_COUNT // 8
    switch_count = max(1, HEAD_COUNT // 8)
    ranking = jax.random.permutation(pieces[0], HEAD_COUNT)
    fast = ranking < fast_count
    switching = (ranking >= fast_count) & (ranking < fast_count + switch_count)
    switch_at = jax.random.randint(pieces[6], (HEAD_COUNT,), TOK_DEV, TOKEN_COUNT - TOK_DEV + 1)
    late = jnp.arange(TOKEN_COUNT)[:, None] >= switch_at[None, :]
    use_fast = fast[None, :] | switching[None, :] & late
    jitter = jnp.exp(jax.random.uniform(pieces[1], (TOKEN_COUNT, HEAD_COUNT), jnp.float32, -math.log(2.0), math.log(2.0)))
    fast_rate = jnp.exp(jax.random.uniform(pieces[2], (HEAD_COUNT,), jnp.float32, math.log(1.0 / 50.0), math.log(1.0 / 30.0)))
    slow_low = math.log(1.0 / TOKEN_COUNT)
    slow_high = math.log(max(1.0 / (4.0 * TOK_DEV), 1.0 / TOKEN_COUNT))
    slow_rate = jnp.exp(jax.random.uniform(pieces[5], (HEAD_COUNT,), jnp.float32, slow_low, slow_high))
    rate = jnp.where(use_fast, fast_rate[None, :], slow_rate[None, :])
    constant_decay = -rate * jitter
    positions = jax.random.randint(pieces[3], (4, HEAD_COUNT), 0, TOKEN_COUNT)
    decay_applied = jnp.any(jnp.arange(TOKEN_COUNT)[:, None, None] == positions[None], axis=1)
    sudden_decay = jnp.log(jax.random.uniform(pieces[4], (TOKEN_COUNT, HEAD_COUNT), jnp.float32, 0.5, 0.8))
    return jnp.where(decay_applied, sudden_decay, constant_decay).astype(jnp.float32)


def block_levels(rng, shape, shards, least, high):
    level, own = 1.0, jax.random.fold_in(rng, 6)
    for position, blocks in shards:
        draws = jnp.exp(jax.random.uniform(jax.random.fold_in(own, position), (blocks,), jnp.float32, least / len(shards), high / len(shards)))
        level = level * jnp.repeat(draws, shape[position] // blocks).reshape([-1 if axis == position else 1 for axis in range(len(shape))])
    return level


def normal_values(own_key, extent, spread, most, cuts=(), held_as=jnp.bfloat16):
    level = block_levels(own_key, extent, cuts, -0.22, 0.18) if cuts else 1.0
    values = jax.random.normal(own_key, extent, jnp.float32) * spread * level
    return jnp.minimum(jnp.maximum(values, -most), most).astype(held_as)


def setup_inputs(seed: int = 0) -> dict:
    key_list = jax.random.split(jax.random.key(seed), 6)
    return {
        "queries": draw_queries(jax.random.fold_in(key_list[5], 71), 0),
        "keys": draw_keys(jax.random.fold_in(key_list[5], 71), 0),
        "values": normal_values(key_list[2], (TOKEN_COUNT, WIDTH), 1.0, 6.0, ((0, 128), (1, 4))),
        "log_decay": draw_log_decay(jax.random.fold_in(key_list[5], 71), 0),
        "norm_gain": jnp.clip(1.0 + 0.18 * jax.random.normal(key_list[4], (WIDTH,), jnp.float32), 0.1, 1.9),
    }


def reference(queries, keys, values, log_decay, norm_gain):
    blocks = TOKEN_COUNT // TOK_DEV
    qb = queries.reshape(blocks, TOK_DEV, HEAD_COUNT, HEAD_DIM)
    kb = keys.reshape(blocks, TOK_DEV, HEAD_COUNT, HEAD_DIM)
    vb = values.reshape(blocks, TOK_DEV, HEAD_COUNT, HEAD_DIM)
    gb = log_decay.reshape(blocks, TOK_DEV, HEAD_COUNT)
    gains = norm_gain.reshape(HEAD_COUNT, HEAD_DIM)
    rows = jnp.arange(TOK_DEV)
    causal = rows[:, None] >= rows[None, :]

    def single_block(state, pieces):
        qh, kh, vh, gates = pieces
        cum = jnp.cumsum(gates, axis=0)
        cum_t = cum.T
        diff = cum_t[:, :, None] - cum_t[:, None, :]
        factor = jnp.where(causal[None], jnp.exp(jnp.minimum(diff, 0.0)), 0.0)
        scores = jnp.einsum('thd,uhd->htu', qh.astype(jnp.float32), kh.astype(jnp.float32))
        weights = (scores * factor).astype(jnp.bfloat16)
        inner = jnp.einsum('htu,uhd->thd', weights.astype(jnp.float32), vh.astype(jnp.float32))
        prior_rounded = state.astype(jnp.bfloat16)
        outer = jnp.einsum('thd,hde->the', qh.astype(jnp.float32), prior_rounded.astype(jnp.float32))
        mixed = inner + outer * jnp.exp(cum)[:, :, None]
        scale = lax.rsqrt(lax.optimization_barrier(jnp.mean(mixed * mixed, axis=-1, keepdims=True)) + 1e-05)
        normed = (mixed * scale * gains[None]).astype(jnp.bfloat16)
        last = cum[-1]
        scaled_keys = (kh.astype(jnp.float32) * jnp.exp(last[None, :] - cum)[:, :, None]).astype(jnp.bfloat16)
        block_state = jnp.einsum('thd,the->hde', scaled_keys.astype(jnp.float32), vh.astype(jnp.float32))
        new_state = jnp.exp(last)[:, None, None] * state + block_state
        return (new_state, normed.reshape(TOK_DEV, WIDTH))
    start = jnp.zeros((HEAD_COUNT, HEAD_DIM, HEAD_DIM), jnp.float32)
    final_state, outputs = lax.scan(single_block, start, (qb, kb, vb, gb))
    return outputs.reshape(TOKEN_COUNT, WIDTH)
```

```python
import functools

import jax
import jax.numpy as jnp
from jax import lax
from jax.experimental import pallas as pl
from jax.experimental.pallas import tpu as pltpu
from jax.sharding import Mesh, PartitionSpec as P

HEAD_DIM = 128
F32 = jnp.float32
B16 = jnp.bfloat16
EXTRA = 16
GROUP = ("zl", "x", "c")


def pieces3(a):
    hi = a.astype(B16)
    rest = a - hi.astype(F32)
    mid = rest.astype(B16)
    return hi, mid, (rest - mid.astype(F32)).astype(B16)


def triangle(n):
    r = lax.broadcasted_iota(jnp.int32, (n, n), 0)
    c = lax.broadcasted_iota(jnp.int32, (n, n), 1)
    return r >= c


def cumulative(g):
    low = triangle(g.shape[0]).astype(F32).astype(B16)
    hi, mid, lo = (jnp.dot(low, p, preferred_element_type=F32) for p in pieces3(g))
    return hi + (mid + lo)


def decay_rows(d):
    d = jnp.broadcast_to(d, (EXTRA, HEAD_DIM))
    hi, mid, lo = (p.astype(F32) for p in pieces3(d))
    row = lax.broadcasted_iota(jnp.int32, d.shape, 0)
    out = jnp.where(row == 0, hi, jnp.where(row == 1, mid, jnp.where(row == 2, lo, 0.0)))
    return out.astype(B16)


def read_decay(rows):
    r = rows.astype(F32)
    return r[0:1] + (r[1:2] + r[2:3])


def states_kernel(k_ref, v_ref, g_ref, o_ref):
    heads = g_ref.shape[1]
    half = o_ref.shape[1] - EXTRA
    cuts = HEAD_DIM // half
    cum = cumulative(g_ref[...])
    last = cum[-1:]
    to_end = jnp.exp(last - cum)
    whole = jnp.exp(last)
    for h in range(heads):
        cols = slice(h * HEAD_DIM, (h + 1) * HEAD_DIM)
        scaled = (k_ref[:, cols].astype(F32) * to_end[:, h : h + 1]).astype(B16)
        state = lax.dot_general(
            scaled, v_ref[:, cols], (((0,), (0,)), ((), ())), preferred_element_type=F32
        ).astype(B16)
        rows = decay_rows(whole[:, h : h + 1])
        for i in range(cuts):
            o_ref[h * cuts + i, :half] = state[i * half : (i + 1) * half]
            o_ref[h * cuts + i, half:] = rows


def total_kernel(x_ref, o_ref):
    n, rows, _ = x_ref.shape
    half = rows - EXTRA
    state = x_ref[0, :half].astype(F32)
    decay = read_decay(x_ref[0, half:])
    for b in range(1, n):
        d = read_decay(x_ref[b, half:])
        state = d * state + x_ref[b, :half].astype(F32)
        decay = decay * d
    state = state.astype(B16)
    tail = decay_rows(decay)
    for j in range(o_ref.shape[0]):
        o_ref[j, :half] = state
        o_ref[j, half:] = tail


def prior_kernel(place_ref, z_ref, x_ref, o_ref):
    place = place_ref[0]
    n, half, _ = o_ref.shape
    state = jnp.zeros((half, HEAD_DIM), F32)
    for j in range(z_ref.shape[0] - 1):
        later = read_decay(z_ref[j, half:]) * state + z_ref[j, :half].astype(F32)
        state = jnp.where(j < place, later, state)
    for b in range(n):
        o_ref[b] = state.astype(B16)
        if b < n - 1:
            state = read_decay(x_ref[b, half:]) * state + x_ref[b, :half].astype(F32)


def inner_kernel(q_ref, k_ref, v_ref, g_ref, gt_ref, o_ref):
    heads = g_ref.shape[1]
    tok = g_ref.shape[0]
    cum = cumulative(g_ref[...])
    up = triangle(tok).astype(F32).astype(B16)
    cum_t = sum(
        lax.dot_general(p, up, (((1,), (1,)), ((), ())), preferred_element_type=F32)
        for p in pieces3(gt_ref[...])[::-1]
    )
    causal = triangle(tok)
    for h in range(heads):
        cols = slice(h * HEAD_DIM, (h + 1) * HEAD_DIM)
        scores = lax.dot_general(
            q_ref[:, cols], k_ref[:, cols], (((1,), (1,)), ((), ())), preferred_element_type=F32
        )
        diff = cum[:, h : h + 1] - cum_t[h : h + 1, :]
        factor = jnp.where(causal, jnp.exp(jnp.minimum(diff, 0.0)), 0.0)
        weights = (scores * factor).astype(B16)
        o_ref[:, cols] = jnp.dot(weights, v_ref[:, cols], preferred_element_type=F32)


def output_kernel(q_ref, s_ref, i_ref, g_ref, gain_ref, o_ref):
    heads = g_ref.shape[1]
    grown = jnp.exp(cumulative(g_ref[...]))
    for h in range(heads):
        cols = slice(h * HEAD_DIM, (h + 1) * HEAD_DIM)
        outer = jnp.dot(q_ref[:, cols], s_ref[h], preferred_element_type=F32)
        mixed = i_ref[:, cols] + outer * grown[:, h : h + 1]
        mean = jnp.mean(mixed * mixed, axis=-1, keepdims=True)
        o_ref[:, cols] = (mixed * lax.rsqrt(mean + 1e-05) * gain_ref[:, cols]).astype(B16)


def local(kernel, shape, dtype, *args, flops=0, smem_first=False):
    specs = [pl.BlockSpec(memory_space=pltpu.VMEM)] * len(args)
    if smem_first:
        specs[0] = pl.BlockSpec(memory_space=pltpu.SMEM)
    moved = sum(a.size * a.dtype.itemsize for a in args)
    return pl.pallas_call(
        kernel,
        out_shape=jax.ShapeDtypeStruct(shape, dtype),
        in_specs=specs,
        out_specs=pl.BlockSpec(memory_space=pltpu.VMEM),
        compiler_params=pltpu.CompilerParams(vmem_limit_bytes=32 * 2**20),
        cost_estimate=pl.CostEstimate(flops=flops, bytes_accessed=moved, transcendentals=0),
    )(*args)


def body(groups, members, queries, keys, values, log_decay, norm_gain):
    tok, width = queries.shape
    heads = log_decay.shape[1]
    half = heads * HEAD_DIM // members
    mac = 2 * heads * tok * HEAD_DIM * HEAD_DIM
    own = local(states_kernel, (members, half + EXTRA, HEAD_DIM), B16, keys, values, log_decay, flops=mac)
    blocks = lax.all_to_all(own, GROUP, 0, 0, tiled=True)
    total = local(total_kernel, (groups, half + EXTRA, HEAD_DIM), B16, blocks)
    totals = lax.all_to_all(total, "zh", 0, 0, tiled=True)
    place = lax.axis_index("zh").astype(jnp.int32).reshape(1)
    prior = local(prior_kernel, (members, half, HEAD_DIM), B16, place, totals, blocks, smem_first=True)
    state = lax.all_to_all(prior, GROUP, 0, 0, tiled=True).reshape(heads, HEAD_DIM, HEAD_DIM)
    inner = local(
        inner_kernel, (tok, width), F32, queries, keys, values, log_decay, log_decay.T, flops=2 * mac
    )
    normed = local(
        output_kernel,
        (tok, width),
        B16,
        queries,
        state,
        inner,
        log_decay,
        norm_gain.reshape(1, width),
        flops=mac,
    )
    return lax.all_to_all(normed, "y", 0, 1, tiled=True)


def solution(mesh):
    seq, mp = mesh.devices.shape
    fine = Mesh(mesh.devices.reshape(seq // 16, 2, 4, 2, mp), ("zh", "zl", "x", "c", "y"))
    tokens = ("zh", "zl", "x", "c")
    in_specs = (P(tokens, "y"),) * 4 + (P("y"),)
    return jax.shard_map(
        functools.partial(body, seq // 16, 16),
        mesh=fine,
        in_specs=in_specs,
        out_specs=P((*tokens, "y"), None),
        check_vma=False,
    )
```

```python
import functools

import jax
import jax.numpy as jnp
from jax import lax
from jax.experimental import pallas as pl
from jax.experimental.pallas import tpu as pltpu
from jax.sharding import Mesh, PartitionSpec as P

HEAD_DIM = 128
F32 = jnp.float32
B16 = jnp.bfloat16
EXTRA = 16


def pieces3(a):
    hi = a.astype(B16)
    rest = a - hi.astype(F32)
    mid = rest.astype(B16)
    return hi, mid, (rest - mid.astype(F32)).astype(B16)


def triangle(n):
    r = lax.broadcasted_iota(jnp.int32, (n, n), 0)
    c = lax.broadcasted_iota(jnp.int32, (n, n), 1)
    return r >= c


def cumulative(gt, columns):
    low = triangle(gt.shape[1]).astype(F32).astype(B16)
    hi, mid, lo = (
        lax.dot_general(
            low if columns else p,
            p if columns else low,
            (((1,), (1,)), ((), ())),
            preferred_element_type=F32,
        )
        for p in pieces3(gt)
    )
    return hi + (mid + lo)


def decay_rows(d):
    d = jnp.broadcast_to(d, (EXTRA, HEAD_DIM))
    hi, mid, lo = (p.astype(F32) for p in pieces3(d))
    row = lax.broadcasted_iota(jnp.int32, d.shape, 0)
    out = jnp.where(row == 0, hi, jnp.where(row == 1, mid, jnp.where(row == 2, lo, 0.0)))
    return out.astype(B16)


def read_decay(rows):
    r = rows.astype(F32)
    return r[0:1] + (r[1:2] + r[2:3])


def states_kernel(k_hbm, v_hbm, g_hbm, o_hbm, k_ref, v_ref, g_ref, o_ref, sems, out_sems):
    heads = g_ref.shape[0]
    half = o_ref.shape[1] - EXTRA
    cuts = HEAD_DIM // half
    gates, *copies = [
        pltpu.make_async_copy(g_hbm, g_ref, sems.at[0]),
        pltpu.make_async_copy(k_hbm, k_ref, sems.at[1]),
        pltpu.make_async_copy(v_hbm, v_ref, sems.at[2]),
    ]
    for copy in (gates, *copies):
        copy.start()
    gates.wait()
    cum = cumulative(g_ref[...], True)
    last = cum[-1:]
    to_end = jnp.exp(last - cum)
    whole = jnp.exp(last)
    for copy in copies:
        copy.wait()
    leaving = []
    for h in range(heads):
        cols = slice(h * HEAD_DIM, (h + 1) * HEAD_DIM)
        scaled = (k_ref[:, cols].astype(F32) * to_end[:, h : h + 1]).astype(B16)
        state = lax.dot_general(
            scaled, v_ref[:, cols], (((0,), (0,)), ((), ())), preferred_element_type=F32
        ).astype(B16)
        rows = decay_rows(whole[:, h : h + 1])
        for i in range(cuts):
            o_ref[h * cuts + i, :half] = state[i * half : (i + 1) * half]
            o_ref[h * cuts + i, half:] = rows
        part = pl.ds(h * cuts, cuts)
        leaving.append(pltpu.make_async_copy(o_ref.at[part], o_hbm.at[part], out_sems.at[h]))
        leaving[-1].start()
    for copy in leaving:
        copy.wait()


def total_kernel(order, x_ref, o_ref):
    n, rows, _ = x_ref.shape
    half = rows - EXTRA
    for b in range(n):
        at = order.index(b)
        d = read_decay(x_ref[at, half:])
        s = x_ref[at, :half].astype(F32)
        state = d * state + s if b else s
        decay = decay * d if b else d
    state = state.astype(B16)
    tail = decay_rows(decay)
    for j in range(o_ref.shape[0]):
        o_ref[j, :half] = state
        o_ref[j, half:] = tail


def prior_kernel(z_order, order, place_ref, z_ref, x_ref, o_ref):
    place = place_ref[0]
    n, half, _ = o_ref.shape
    state = jnp.zeros((half, HEAD_DIM), F32)
    for j in range(z_ref.shape[0] - 1):
        at = z_order.index(j)
        later = read_decay(z_ref[at, half:]) * state + z_ref[at, :half].astype(F32)
        state = jnp.where(j < place, later, state)
    for b in range(n):
        at = order.index(b)
        o_ref[at] = state.astype(B16)
        if b < n - 1:
            state = read_decay(x_ref[at, half:]) * state + x_ref[at, :half].astype(F32)


def inner_kernel(q_ref, k_ref, v_ref, g_ref, o_ref):
    heads, tok = g_ref.shape
    cum = cumulative(g_ref[...], True)
    cum_t = cumulative(g_ref[...], False)
    causal = triangle(tok)
    for h in range(heads):
        cols = slice(h * HEAD_DIM, (h + 1) * HEAD_DIM)
        scores = lax.dot_general(
            q_ref[:, cols], k_ref[:, cols], (((1,), (1,)), ((), ())), preferred_element_type=F32
        )
        diff = cum[:, h : h + 1] - cum_t[h : h + 1, :]
        factor = jnp.where(causal, jnp.exp(jnp.minimum(diff, 0.0)), 0.0)
        weights = (scores * factor).astype(B16)
        o_ref[:, cols] = jnp.dot(weights, v_ref[:, cols], preferred_element_type=F32)


def output_kernel(order, q_ref, s_ref, i_ref, g_ref, gain_ref, o_ref):
    heads = g_ref.shape[0]
    grown = jnp.exp(cumulative(g_ref[...], True))
    for h in range(heads):
        cols = slice(h * HEAD_DIM, (h + 1) * HEAD_DIM)
        outer = jnp.dot(q_ref[:, cols], s_ref[h], preferred_element_type=F32)
        mixed = i_ref[:, cols] + outer * grown[:, h : h + 1]
        mean = jnp.mean(mixed * mixed, axis=-1, keepdims=True)
        normed = (mixed * lax.rsqrt(mean + 1e-05) * gain_ref[:, cols]).astype(B16)
        quarter = o_ref.shape[1]
        for j, place in enumerate(order):
            o_ref[j, :, cols] = normed[place * quarter : (place + 1) * quarter]


def local(kernel, shape, dtype, *args, flops=0, spaces=(), out=pltpu.VMEM, scratch=(), vmem=32):
    spaces = (*spaces, *(pltpu.VMEM,) * (len(args) - len(spaces)))
    moved = sum(a.size * a.dtype.itemsize for a in args)
    return pl.pallas_call(
        kernel,
        out_shape=jax.ShapeDtypeStruct(shape, dtype),
        in_specs=[pl.BlockSpec(memory_space=space) for space in spaces],
        out_specs=pl.BlockSpec(memory_space=out),
        scratch_shapes=scratch,
        compiler_params=pltpu.CompilerParams(vmem_limit_bytes=vmem * 2**20),
        cost_estimate=pl.CostEstimate(flops=flops, bytes_accessed=moved, transcendentals=0),
    )(*args)


def rotated(n, first):
    return [(first + j) % n for j in range(n)]


def exchange(a, axis, order):
    return lax.all_to_all(a, axis, 0, 0, tiled=True, axis_index_groups=[order])


def body(groups, members, queries, keys, values, log_decay, norm_gain):
    tok, width = queries.shape
    heads = log_decay.shape[1]
    mps = lax.axis_size("mp")
    half = heads * HEAD_DIM // members
    mac = 2 * heads * tok * HEAD_DIM * HEAD_DIM
    z_order = rotated(groups, (5 * groups) // 8)
    order = rotated(members, (13 * members) // 16)
    y_order = rotated(mps, mps // 2)
    gates = log_decay.T
    own = local(
        states_kernel,
        (members, half + EXTRA, HEAD_DIM),
        B16,
        keys,
        values,
        gates,
        flops=mac,
        spaces=(pl.ANY,) * 3,
        out=pl.ANY,
        scratch=[
            pltpu.VMEM((tok, width), B16),
            pltpu.VMEM((tok, width), B16),
            pltpu.VMEM((heads, tok), F32),
            pltpu.VMEM((members, half + EXTRA, HEAD_DIM), B16),
            pltpu.SemaphoreType.DMA((3,)),
            pltpu.SemaphoreType.DMA((heads,)),
        ],
        vmem=60,
    )
    blocks = exchange(own, "g", order)
    total = local(
        functools.partial(total_kernel, order), (groups, half + EXTRA, HEAD_DIM), B16, blocks
    )
    totals = exchange(total, "zh", z_order)
    place = lax.axis_index("zh").astype(jnp.int32).reshape(1)
    prior = local(
        functools.partial(prior_kernel, z_order, order),
        (members, half, HEAD_DIM),
        B16,
        place,
        totals,
        blocks,
        spaces=(pltpu.SMEM,),
    )
    state = exchange(prior, "g", order).reshape(heads, HEAD_DIM, HEAD_DIM)
    inner = local(
        inner_kernel, (tok, width), F32, queries, keys, values, gates, flops=2 * mac
    )
    normed = local(
        functools.partial(output_kernel, y_order),
        (mps, tok // mps, width),
        B16,
        queries,
        state,
        inner,
        gates,
        norm_gain.reshape(1, width),
        flops=mac,
    )
    arrived = exchange(normed, "mp", y_order)
    return jnp.concatenate([arrived[y_order.index(y)] for y in range(mps)], axis=1)


def solution(mesh):
    seq, mp = mesh.devices.shape
    fine = Mesh(mesh.devices.reshape(seq // 16, 16, mp), ("zh", "g", "mp"))
    in_specs = (P(("zh", "g"), "mp"),) * 4 + (P("mp"),)
    return jax.shard_map(
        functools.partial(body, seq // 16, 16),
        mesh=fine,
        in_specs=in_specs,
        out_specs=P(("zh", "g", "mp"), None),
        check_vma=False,
    )
```

```python
import functools

import jax
import jax.numpy as jnp
from jax import lax
from jax.experimental import pallas as pl
from jax.experimental.pallas import tpu as pltpu
from jax.sharding import Mesh, PartitionSpec as P

HEAD_DIM = 128
F32 = jnp.float32
B16 = jnp.bfloat16
EXTRA = 8


def pieces3(a):
    hi = a.astype(B16)
    rest = a - hi.astype(F32)
    mid = rest.astype(B16)
    return hi, mid, (rest - mid.astype(F32)).astype(B16)


def triangle(n):
    r = lax.broadcasted_iota(jnp.int32, (n, n), 0)
    c = lax.broadcasted_iota(jnp.int32, (n, n), 1)
    return r >= c


def cumulative(gt, columns):
    low = triangle(gt.shape[1]).astype(F32).astype(B16)
    hi, mid, lo = (
        lax.dot_general(
            low if columns else p,
            p if columns else low,
            (((1,), (1,)), ((), ())),
            preferred_element_type=F32,
        )
        for p in pieces3(gt)
    )
    return hi + (mid + lo)


def decay_rows(d):
    d = jnp.broadcast_to(d, (EXTRA, HEAD_DIM))
    hi, mid, lo = (p.astype(F32) for p in pieces3(d))
    row = lax.broadcasted_iota(jnp.int32, d.shape, 0)
    out = jnp.where(row == 0, hi, jnp.where(row == 1, mid, jnp.where(row == 2, lo, 0.0)))
    return out.astype(B16)


def read_decay(rows):
    r = rows.astype(F32)
    return r[0:1] + (r[1:2] + r[2:3])


def states_kernel(k_hbm, v_hbm, g_hbm, o_hbm, k_ref, v_ref, g_ref, o_ref, sems, out_sems):
    heads = g_ref.shape[0]
    half = o_ref.shape[1] - EXTRA
    cuts = HEAD_DIM // half
    gates, *copies = [
        pltpu.make_async_copy(g_hbm, g_ref, sems.at[0]),
        pltpu.make_async_copy(k_hbm, k_ref, sems.at[1]),
        pltpu.make_async_copy(v_hbm, v_ref, sems.at[2]),
    ]
    for copy in (gates, *copies):
        copy.start()
    gates.wait()
    cum = cumulative(g_ref[...], True)
    last = cum[-1:]
    to_end = jnp.exp(last - cum)
    whole = jnp.exp(last)
    for copy in copies:
        copy.wait()
    leaving = []
    for h in range(heads):
        cols = slice(h * HEAD_DIM, (h + 1) * HEAD_DIM)
        scaled = (k_ref[:, cols].astype(F32) * to_end[:, h : h + 1]).astype(B16)
        state = lax.dot_general(
            scaled, v_ref[:, cols], (((0,), (0,)), ((), ())), preferred_element_type=F32
        ).astype(B16)
        rows = decay_rows(whole[:, h : h + 1])
        for i in range(cuts):
            o_ref[h * cuts + i, :half] = state[i * half : (i + 1) * half]
            o_ref[h * cuts + i, half:] = rows
        part = pl.ds(h * cuts, cuts)
        leaving.append(pltpu.make_async_copy(o_ref.at[part], o_hbm.at[part], out_sems.at[h]))
        leaving[-1].start()
    for copy in leaving:
        copy.wait()


def total_kernel(order, x_ref, o_ref):
    n, rows, _ = x_ref.shape
    half = rows - EXTRA
    for b in range(n):
        at = order.index(b)
        d = read_decay(x_ref[at, half:])
        s = x_ref[at, :half].astype(F32)
        state = d * state + s if b else s
        decay = decay * d if b else d
    state = state.astype(B16)
    tail = decay_rows(decay)
    for j in range(o_ref.shape[0]):
        o_ref[j, :half] = state
        o_ref[j, half:] = tail


def prior_kernel(z_order, order, place_ref, z_ref, x_ref, o_ref):
    place = place_ref[0]
    n, half, _ = o_ref.shape
    state = jnp.zeros((half, HEAD_DIM), F32)
    for j in range(z_ref.shape[0] - 1):
        at = z_order.index(j)
        later = read_decay(z_ref[at, half:]) * state + z_ref[at, :half].astype(F32)
        state = jnp.where(j < place, later, state)
    for b in range(n):
        at = order.index(b)
        o_ref[at] = state.astype(B16)
        if b < n - 1:
            state = read_decay(x_ref[at, half:]) * state + x_ref[at, :half].astype(F32)


def inner_kernel(q_ref, k_ref, v_ref, g_ref, o_ref):
    heads, tok = g_ref.shape
    cum = cumulative(g_ref[...], True)
    cum_t = cumulative(g_ref[...], False)
    causal = triangle(tok)
    for h in range(heads):
        cols = slice(h * HEAD_DIM, (h + 1) * HEAD_DIM)
        scores = lax.dot_general(
            q_ref[:, cols], k_ref[:, cols], (((1,), (1,)), ((), ())), preferred_element_type=F32
        )
        diff = cum[:, h : h + 1] - cum_t[h : h + 1, :]
        factor = jnp.where(causal, jnp.exp(jnp.minimum(diff, 0.0)), 0.0)
        weights = (scores * factor).astype(B16)
        o_ref[:, cols] = jnp.dot(weights, v_ref[:, cols], preferred_element_type=F32)


def output_kernel(order, q_ref, s_ref, i_ref, g_ref, gain_ref, o_ref):
    heads = g_ref.shape[0]
    grown = jnp.exp(cumulative(g_ref[...], True))
    for h in range(heads):
        cols = slice(h * HEAD_DIM, (h + 1) * HEAD_DIM)
        outer = jnp.dot(q_ref[:, cols], s_ref[h], preferred_element_type=F32)
        mixed = i_ref[:, cols] + outer * grown[:, h : h + 1]
        mean = jnp.mean(mixed * mixed, axis=-1, keepdims=True)
        normed = (mixed * lax.rsqrt(mean + 1e-05) * gain_ref[:, cols]).astype(B16)
        quarter = o_ref.shape[1]
        for j, place in enumerate(order):
            o_ref[j, :, cols] = normed[place * quarter : (place + 1) * quarter]


def local(kernel, shape, dtype, *args, flops=0, spaces=(), out=pltpu.VMEM, scratch=(), vmem=32):
    spaces = (*spaces, *(pltpu.VMEM,) * (len(args) - len(spaces)))
    moved = sum(a.size * a.dtype.itemsize for a in args)
    return pl.pallas_call(
        kernel,
        out_shape=jax.ShapeDtypeStruct(shape, dtype),
        in_specs=[pl.BlockSpec(memory_space=space) for space in spaces],
        out_specs=pl.BlockSpec(memory_space=out),
        scratch_shapes=scratch,
        compiler_params=pltpu.CompilerParams(vmem_limit_bytes=vmem * 2**20),
        cost_estimate=pl.CostEstimate(flops=flops, bytes_accessed=moved, transcendentals=0),
    )(*args)


def rotated(n, first):
    return [(first + j) % n for j in range(n)]


def exchange(a, axis, order):
    return lax.all_to_all(a, axis, 0, 0, tiled=True, axis_index_groups=[order])


def body(groups, members, queries, keys, values, log_decay, norm_gain):
    tok, width = queries.shape
    heads = log_decay.shape[1]
    mps = lax.axis_size("mp")
    half = heads * HEAD_DIM // members
    mac = 2 * heads * tok * HEAD_DIM * HEAD_DIM
    z_order = [(5 * groups) // 8]
    z_order += [z for z in range(groups)[::-1] if z not in z_order]
    order = rotated(members, (13 * members) // 16)
    y_order = rotated(mps, mps // 2)
    gates = log_decay.T
    own = local(
        states_kernel,
        (members, half + EXTRA, HEAD_DIM),
        B16,
        keys,
        values,
        gates,
        flops=mac,
        spaces=(pl.ANY,) * 3,
        out=pl.ANY,
        scratch=[
            pltpu.VMEM((tok, width), B16),
            pltpu.VMEM((tok, width), B16),
            pltpu.VMEM((heads, tok), F32),
            pltpu.VMEM((members, half + EXTRA, HEAD_DIM), B16),
            pltpu.SemaphoreType.DMA((3,)),
            pltpu.SemaphoreType.DMA((heads,)),
        ],
        vmem=60,
    )
    blocks = exchange(own, "g", order)
    total = local(
        functools.partial(total_kernel, order), (groups, half + EXTRA, HEAD_DIM), B16, blocks
    )
    totals = exchange(total, "zh", z_order)
    place = lax.axis_index("zh").astype(jnp.int32).reshape(1)
    inner = local(
        inner_kernel, (tok, width), F32, queries, keys, values, gates, flops=2 * mac
    )
    totals, inner = lax.optimization_barrier((totals, inner))
    prior = local(
        functools.partial(prior_kernel, z_order, order),
        (members, half, HEAD_DIM),
        B16,
        place,
        totals,
        blocks,
        spaces=(pltpu.SMEM,),
    )
    state = exchange(prior, "g", order).reshape(heads, HEAD_DIM, HEAD_DIM)
    normed = local(
        functools.partial(output_kernel, y_order),
        (mps, tok // mps, width),
        B16,
        queries,
        state,
        inner,
        gates,
        norm_gain.reshape(1, width),
        flops=mac,
    )
    arrived = exchange(normed, "mp", y_order)
    return jnp.concatenate([arrived[y_order.index(y)] for y in range(mps)], axis=1)


def solution(mesh):
    seq, mp = mesh.devices.shape
    fine = Mesh(mesh.devices.reshape(seq // 16, 16, mp), ("zh", "g", "mp"))
    in_specs = (P(("zh", "g"), "mp"),) * 4 + (P("mp"),)
    return jax.shard_map(
        functools.partial(body, seq // 16, 16),
        mesh=fine,
        in_specs=in_specs,
        out_specs=P(("zh", "g", "mp"), None),
        check_vma=False,
    )
```

```python
import functools

import jax
import jax.numpy as jnp
from jax import lax
from jax.experimental import pallas as pl
from jax.experimental.pallas import tpu as pltpu
from jax.sharding import Mesh, PartitionSpec as P

HEAD_DIM = 128
F32 = jnp.float32
B16 = jnp.bfloat16
EXTRA = 8


def pieces3(a):
    hi = a.astype(B16)
    rest = a - hi.astype(F32)
    mid = rest.astype(B16)
    return hi, mid, (rest - mid.astype(F32)).astype(B16)


def triangle(n):
    r = lax.broadcasted_iota(jnp.int32, (n, n), 0)
    c = lax.broadcasted_iota(jnp.int32, (n, n), 1)
    return r >= c


def cumulative(gt, columns):
    low = triangle(gt.shape[1]).astype(F32).astype(B16)
    hi, mid, lo = (
        lax.dot_general(
            low if columns else p,
            p if columns else low,
            (((1,), (1,)), ((), ())),
            preferred_element_type=F32,
        )
        for p in pieces3(gt)
    )
    return hi + (mid + lo)


def decay_rows(d):
    d = jnp.broadcast_to(d, (EXTRA, HEAD_DIM))
    hi, mid, lo = (p.astype(F32) for p in pieces3(d))
    row = lax.broadcasted_iota(jnp.int32, d.shape, 0)
    out = jnp.where(row == 0, hi, jnp.where(row == 1, mid, jnp.where(row == 2, lo, 0.0)))
    return out.astype(B16)


def read_decay(rows):
    r = rows.astype(F32)
    return r[0:1] + (r[1:2] + r[2:3])


def states_kernel(k_hbm, v_hbm, g_hbm, o_hbm, k_ref, v_ref, g_ref, o_ref, sems, out_sems):
    heads = g_ref.shape[0]
    half = o_ref.shape[1] - EXTRA
    cuts = HEAD_DIM // half
    gates, *copies = [
        pltpu.make_async_copy(g_hbm, g_ref, sems.at[0]),
        pltpu.make_async_copy(k_hbm, k_ref, sems.at[1]),
        pltpu.make_async_copy(v_hbm, v_ref, sems.at[2]),
    ]
    for copy in (gates, *copies):
        copy.start()
    gates.wait()
    cum = cumulative(g_ref[...], True)
    last = cum[-1:]
    to_end = jnp.exp(last - cum)
    whole = jnp.exp(last)
    for copy in copies:
        copy.wait()
    leaving = []
    for h in range(heads):
        cols = slice(h * HEAD_DIM, (h + 1) * HEAD_DIM)
        scaled = (k_ref[:, cols].astype(F32) * to_end[:, h : h + 1]).astype(B16)
        state = lax.dot_general(
            scaled, v_ref[:, cols], (((0,), (0,)), ((), ())), preferred_element_type=F32
        ).astype(B16)
        rows = decay_rows(whole[:, h : h + 1])
        for i in range(cuts):
            o_ref[h * cuts + i, :half] = state[i * half : (i + 1) * half]
            o_ref[h * cuts + i, half:] = rows
        part = pl.ds(h * cuts, cuts)
        leaving.append(pltpu.make_async_copy(o_ref.at[part], o_hbm.at[part], out_sems.at[h]))
        leaving[-1].start()
    for copy in leaving:
        copy.wait()


def total_kernel(order, x_ref, o_ref, d_ref):
    n, rows, _ = x_ref.shape
    half = rows - EXTRA
    for b in range(n):
        at = order.index(b)
        d = read_decay(x_ref[at, half:])
        d_ref[b : b + 1] = d
        s = x_ref[at, :half].astype(F32)
        state = d * state + s if b else s
        decay = decay * d if b else d
    state = state.astype(B16)
    tail = decay_rows(decay)
    for j in range(o_ref.shape[0]):
        o_ref[j, :half] = state
        o_ref[j, half:] = tail


def prior_kernel(z_order, order, place_ref, z_ref, x_ref, d_ref, o_ref):
    place = place_ref[0]
    n, half, _ = o_ref.shape
    state = jnp.zeros((half, HEAD_DIM), F32)
    for j in range(z_ref.shape[0] - 1):
        at = z_order.index(j)
        later = read_decay(z_ref[at, half:]) * state + z_ref[at, :half].astype(F32)
        state = jnp.where(j < place, later, state)
    for b in range(n):
        at = order.index(b)
        o_ref[at] = state.astype(B16)
        if b < n - 1:
            state = d_ref[b : b + 1] * state + x_ref[at, :half].astype(F32)


def inner_kernel(q_ref, k_ref, v_ref, g_ref, o_ref, e_ref):
    heads, tok = g_ref.shape
    cum = cumulative(g_ref[...], True)
    cum_t = cumulative(g_ref[...], False)
    e_ref[...] = jnp.exp(cum)
    causal = triangle(tok)
    for h in range(heads):
        cols = slice(h * HEAD_DIM, (h + 1) * HEAD_DIM)
        scores = lax.dot_general(
            q_ref[:, cols], k_ref[:, cols], (((1,), (1,)), ((), ())), preferred_element_type=F32
        )
        diff = cum[:, h : h + 1] - cum_t[h : h + 1, :]
        factor = jnp.where(causal, jnp.exp(jnp.minimum(diff, 0.0)), 0.0)
        weights = (scores * factor).astype(B16)
        o_ref[:, cols] = jnp.dot(weights, v_ref[:, cols], preferred_element_type=F32)


def output_kernel(order, q_ref, s_ref, i_ref, e_ref, gain_ref, o_ref):
    heads = e_ref.shape[1]
    grown = e_ref[...]
    for h in range(heads):
        cols = slice(h * HEAD_DIM, (h + 1) * HEAD_DIM)
        outer = jnp.dot(q_ref[:, cols], s_ref[h], preferred_element_type=F32)
        mixed = i_ref[:, cols] + outer * grown[:, h : h + 1]
        mean = jnp.mean(mixed * mixed, axis=-1, keepdims=True)
        normed = (mixed * lax.rsqrt(mean + 1e-05) * gain_ref[:, cols]).astype(B16)
        quarter = o_ref.shape[1]
        for j, place in enumerate(order):
            o_ref[j, :, cols] = normed[place * quarter : (place + 1) * quarter]


def local(kernel, outs, *args, flops=0, spaces=(), out=pltpu.VMEM, scratch=(), vmem=32):
    spaces = (*spaces, *(pltpu.VMEM,) * (len(args) - len(spaces)))
    moved = sum(a.size * a.dtype.itemsize for a in args)
    return pl.pallas_call(
        kernel,
        out_shape=[jax.ShapeDtypeStruct(shape, dtype) for shape, dtype in outs],
        in_specs=[pl.BlockSpec(memory_space=space) for space in spaces],
        out_specs=[pl.BlockSpec(memory_space=out)] * len(outs),
        scratch_shapes=scratch,
        compiler_params=pltpu.CompilerParams(vmem_limit_bytes=vmem * 2**20),
        cost_estimate=pl.CostEstimate(flops=flops, bytes_accessed=moved, transcendentals=0),
    )(*args)


def rotated(n, first):
    return [(first + j) % n for j in range(n)]


def exchange(a, axis, order):
    return lax.all_to_all(a, axis, 0, 0, tiled=True, axis_index_groups=[order])


def body(groups, members, queries, keys, values, log_decay, norm_gain):
    tok, width = queries.shape
    heads = log_decay.shape[1]
    mps = lax.axis_size("mp")
    half = heads * HEAD_DIM // members
    mac = 2 * heads * tok * HEAD_DIM * HEAD_DIM
    z_order = [(5 * groups) // 8]
    z_order += [z for z in range(groups)[::-1] if z not in z_order]
    order = rotated(members, (13 * members) // 16)
    y_order = rotated(mps, mps // 2)
    gates = log_decay.T
    (own,) = local(
        states_kernel,
        [((members, half + EXTRA, HEAD_DIM), B16)],
        keys,
        values,
        gates,
        flops=mac,
        spaces=(pl.ANY,) * 3,
        out=pl.ANY,
        scratch=[
            pltpu.VMEM((tok, width), B16),
            pltpu.VMEM((tok, width), B16),
            pltpu.VMEM((heads, tok), F32),
            pltpu.VMEM((members, half + EXTRA, HEAD_DIM), B16),
            pltpu.SemaphoreType.DMA((3,)),
            pltpu.SemaphoreType.DMA((heads,)),
        ],
        vmem=60,
    )
    blocks = exchange(own, "g", order)
    total, decays = local(
        functools.partial(total_kernel, order),
        [((groups, half + EXTRA, HEAD_DIM), B16), ((members, HEAD_DIM), F32)],
        blocks,
    )
    totals = exchange(total, "zh", z_order)
    place = lax.axis_index("zh").astype(jnp.int32).reshape(1)
    inner, grown = local(
        inner_kernel,
        [((tok, width), F32), ((tok, heads), F32)],
        queries,
        keys,
        values,
        gates,
        flops=2 * mac,
    )
    totals, inner, grown = lax.optimization_barrier((totals, inner, grown))
    (prior,) = local(
        functools.partial(prior_kernel, z_order, order),
        [((members, half, HEAD_DIM), B16)],
        place,
        totals,
        blocks,
        decays,
        spaces=(pltpu.SMEM,),
    )
    state = exchange(prior, "g", order).reshape(heads, HEAD_DIM, HEAD_DIM)
    (normed,) = local(
        functools.partial(output_kernel, y_order),
        [((mps, tok // mps, width), B16)],
        queries,
        state,
        inner,
        grown,
        norm_gain.reshape(1, width),
        flops=mac,
    )
    arrived = exchange(normed, "mp", y_order)
    return jnp.concatenate([arrived[y_order.index(y)] for y in range(mps)], axis=1)


def solution(mesh):
    seq, mp = mesh.devices.shape
    fine = Mesh(mesh.devices.reshape(seq // 16, 16, mp), ("zh", "g", "mp"))
    in_specs = (P(("zh", "g"), "mp"),) * 4 + (P("mp"),)
    return jax.shard_map(
        functools.partial(body, seq // 16, 16),
        mesh=fine,
        in_specs=in_specs,
        out_specs=P(("zh", "g", "mp"), None),
        check_vma=False,
    )
```

```python
import functools

import jax
import jax.numpy as jnp
from jax import lax
from jax.experimental import pallas as pl
from jax.experimental.pallas import tpu as pltpu
from jax.sharding import Mesh, PartitionSpec as P

HEAD_DIM = 128
F32 = jnp.float32
B16 = jnp.bfloat16
EXTRA = 8


def pieces3(a):
    hi = a.astype(B16)
    rest = a - hi.astype(F32)
    mid = rest.astype(B16)
    return hi, mid, (rest - mid.astype(F32)).astype(B16)


def triangle(n):
    r = lax.broadcasted_iota(jnp.int32, (n, n), 0)
    c = lax.broadcasted_iota(jnp.int32, (n, n), 1)
    return r >= c


def cumulative(gt, columns):
    low = triangle(gt.shape[1]).astype(F32).astype(B16)
    hi, mid, lo = (
        lax.dot_general(
            low if columns else p,
            p if columns else low,
            (((1,), (1,)), ((), ())),
            preferred_element_type=F32,
        )
        for p in pieces3(gt)
    )
    return hi + (mid + lo)


def decay_rows(d):
    d = jnp.broadcast_to(d, (EXTRA, HEAD_DIM))
    hi, mid, lo = (p.astype(F32) for p in pieces3(d))
    row = lax.broadcasted_iota(jnp.int32, d.shape, 0)
    out = jnp.where(row == 0, hi, jnp.where(row == 1, mid, jnp.where(row == 2, lo, 0.0)))
    return out.astype(B16)


def read_decay(rows):
    r = rows.astype(F32)
    return r[0:1] + (r[1:2] + r[2:3])


def states_kernel(k_hbm, v_hbm, g_hbm, o_hbm, k_ref, v_ref, g_ref, o_ref, sems, out_sems):
    heads = g_ref.shape[0]
    half = o_ref.shape[1] - EXTRA
    cuts = HEAD_DIM // half
    gates, *copies = [
        pltpu.make_async_copy(g_hbm, g_ref, sems.at[0]),
        pltpu.make_async_copy(k_hbm, k_ref, sems.at[1]),
        pltpu.make_async_copy(v_hbm, v_ref, sems.at[2]),
    ]
    for copy in (gates, *copies):
        copy.start()
    gates.wait()
    cum = cumulative(g_ref[...], True)
    last = cum[-1:]
    to_end = jnp.exp(last - cum)
    whole = jnp.exp(last)
    for copy in copies:
        copy.wait()
    leaving = []
    for h in range(heads):
        cols = slice(h * HEAD_DIM, (h + 1) * HEAD_DIM)
        scaled = (k_ref[:, cols].astype(F32) * to_end[:, h : h + 1]).astype(B16)
        state = lax.dot_general(
            scaled, v_ref[:, cols], (((0,), (0,)), ((), ())), preferred_element_type=F32
        ).astype(B16)
        rows = decay_rows(whole[:, h : h + 1])
        for i in range(cuts):
            o_ref[h * cuts + i, :half] = state[i * half : (i + 1) * half]
            o_ref[h * cuts + i, half:] = rows
        part = pl.ds(h * cuts, cuts)
        leaving.append(pltpu.make_async_copy(o_ref.at[part], o_hbm.at[part], out_sems.at[h]))
        leaving[-1].start()
    for copy in leaving:
        copy.wait()


def total_kernel(order, x_ref, o_ref, d_ref):
    n, rows, _ = x_ref.shape
    half = rows - EXTRA
    for b in range(n):
        at = order.index(b)
        d = read_decay(x_ref[at, half:])
        d_ref[b : b + 1] = d
        s = x_ref[at, :half].astype(F32)
        state = d * state + s if b else s
        decay = decay * d if b else d
    state = state.astype(B16)
    tail = decay_rows(decay)
    for j in range(o_ref.shape[0]):
        o_ref[j, :half] = state
        o_ref[j, half:] = tail


def half_kernel(z_order, z_ref, o_ref):
    half = o_ref.shape[0]
    state = jnp.zeros((half, HEAD_DIM), F32)
    for j in range(z_ref.shape[0]):
        at = z_order.index(j)
        state = read_decay(z_ref[at, half:]) * state + z_ref[at, :half].astype(F32)
    o_ref[...] = state.astype(B16)


def prior_kernel(low_order, high_order, order, place_ref, low_ref, high_ref, first_ref, x_ref, d_ref, o_ref):
    n, half, _ = o_ref.shape
    count = low_ref.shape[0]
    late = place_ref[0] >= count
    place = lax.rem(place_ref[0], count)
    state = jnp.where(late, first_ref[...].astype(F32), 0.0)
    for j in range(count - 1):
        low, high = low_order.index(j), high_order.index(j)
        decay = jnp.where(late, read_decay(high_ref[high, half:]), read_decay(low_ref[low, half:]))
        own = jnp.where(late, high_ref[high, :half].astype(F32), low_ref[low, :half].astype(F32))
        state = jnp.where(j < place, decay * state + own, state)
    for b in range(n):
        at = order.index(b)
        o_ref[at] = state.astype(B16)
        if b < n - 1:
            state = d_ref[b : b + 1] * state + x_ref[at, :half].astype(F32)


def inner_kernel(q_ref, k_ref, v_ref, g_ref, o_ref, e_ref):
    heads, tok = g_ref.shape
    cum = cumulative(g_ref[...], True)
    cum_t = cumulative(g_ref[...], False)
    e_ref[...] = jnp.exp(cum)
    causal = triangle(tok)
    for h in range(heads):
        cols = slice(h * HEAD_DIM, (h + 1) * HEAD_DIM)
        scores = lax.dot_general(
            q_ref[:, cols], k_ref[:, cols], (((1,), (1,)), ((), ())), preferred_element_type=F32
        )
        diff = cum[:, h : h + 1] - cum_t[h : h + 1, :]
        factor = jnp.where(causal, jnp.exp(jnp.minimum(diff, 0.0)), 0.0)
        weights = (scores * factor).astype(B16)
        o_ref[:, cols] = jnp.dot(weights, v_ref[:, cols], preferred_element_type=F32)


def output_kernel(order, q_ref, s_ref, i_ref, e_ref, gain_ref, o_ref):
    heads = e_ref.shape[1]
    grown = e_ref[...]
    for h in range(heads):
        cols = slice(h * HEAD_DIM, (h + 1) * HEAD_DIM)
        outer = jnp.dot(q_ref[:, cols], s_ref[h], preferred_element_type=F32)
        mixed = i_ref[:, cols] + outer * grown[:, h : h + 1]
        mean = jnp.mean(mixed * mixed, axis=-1, keepdims=True)
        normed = (mixed * lax.rsqrt(mean + 1e-05) * gain_ref[:, cols]).astype(B16)
        quarter = o_ref.shape[1]
        for j, place in enumerate(order):
            o_ref[j, :, cols] = normed[place * quarter : (place + 1) * quarter]


def local(kernel, outs, *args, flops=0, spaces=(), out=pltpu.VMEM, scratch=(), vmem=32):
    spaces = (*spaces, *(pltpu.VMEM,) * (len(args) - len(spaces)))
    moved = sum(a.size * a.dtype.itemsize for a in args)
    return pl.pallas_call(
        kernel,
        out_shape=[jax.ShapeDtypeStruct(shape, dtype) for shape, dtype in outs],
        in_specs=[pl.BlockSpec(memory_space=space) for space in spaces],
        out_specs=[pl.BlockSpec(memory_space=out)] * len(outs),
        scratch_shapes=scratch,
        compiler_params=pltpu.CompilerParams(vmem_limit_bytes=vmem * 2**20),
        cost_estimate=pl.CostEstimate(flops=flops, bytes_accessed=moved, transcendentals=0),
    )(*args)


def rotated(n, first):
    return [(first + j) % n for j in range(n)]


def exchange(a, axis, order):
    return lax.all_to_all(a, axis, 0, 0, tiled=True, axis_index_groups=[order])


def body(groups, members, queries, keys, values, log_decay, norm_gain):
    tok, width = queries.shape
    heads = log_decay.shape[1]
    mps = lax.axis_size("mp")
    half = heads * HEAD_DIM // members
    mac = 2 * heads * tok * HEAD_DIM * HEAD_DIM
    count = groups // 2
    low_order = list(range(count))[::-1]
    high_order = [1, *range(count)[:1:-1], 0]
    order = rotated(members, (13 * members) // 16)
    y_order = rotated(mps, mps // 2)
    gates = log_decay.T
    (own,) = local(
        states_kernel,
        [((members, half + EXTRA, HEAD_DIM), B16)],
        keys,
        values,
        gates,
        flops=mac,
        spaces=(pl.ANY,) * 3,
        out=pl.ANY,
        scratch=[
            pltpu.VMEM((tok, width), B16),
            pltpu.VMEM((tok, width), B16),
            pltpu.VMEM((heads, tok), F32),
            pltpu.VMEM((members, half + EXTRA, HEAD_DIM), B16),
            pltpu.SemaphoreType.DMA((3,)),
            pltpu.SemaphoreType.DMA((heads,)),
        ],
        vmem=60,
    )
    blocks = exchange(own, "g", order)
    total, decays = local(
        functools.partial(total_kernel, order),
        [((count, half + EXTRA, HEAD_DIM), B16), ((members, HEAD_DIM), F32)],
        blocks,
    )
    zh = lax.axis_index("zh")
    place = zh.astype(jnp.int32).reshape(1)
    z_groups = [low_order, [count + j for j in high_order]]

    def swap(a):
        return lax.all_to_all(a, "zh", 0, 0, tiled=True, axis_index_groups=z_groups)

    low = lax.cond(zh < count, swap, lambda a: a, total)
    (sent,) = local(functools.partial(half_kernel, low_order), [((half, HEAD_DIM), B16)], low)
    first = lax.ppermute(sent, "zh", [(j, groups - 1 - j) for j in range(count)])
    total, sent = lax.optimization_barrier((total, sent))
    high = lax.cond(zh < count, lambda a: a, swap, total)
    inner, grown = local(
        inner_kernel,
        [((tok, width), F32), ((tok, heads), F32)],
        queries,
        keys,
        values,
        gates,
        flops=2 * mac,
    )
    high, inner, grown = lax.optimization_barrier((high, inner, grown))
    (prior,) = local(
        functools.partial(prior_kernel, low_order, high_order, order),
        [((members, half, HEAD_DIM), B16)],
        place,
        low,
        high,
        first,
        blocks,
        decays,
        spaces=(pltpu.SMEM,),
    )
    state = exchange(prior, "g", order).reshape(heads, HEAD_DIM, HEAD_DIM)
    (normed,) = local(
        functools.partial(output_kernel, y_order),
        [((mps, tok // mps, width), B16)],
        queries,
        state,
        inner,
        grown,
        norm_gain.reshape(1, width),
        flops=mac,
    )
    arrived = exchange(normed, "mp", y_order)
    return jnp.concatenate([arrived[y_order.index(y)] for y in range(mps)], axis=1)


def solution(mesh):
    seq, mp = mesh.devices.shape
    fine = Mesh(mesh.devices.reshape(seq // 16, 16, mp), ("zh", "g", "mp"))
    in_specs = (P(("zh", "g"), "mp"),) * 4 + (P("mp"),)
    return jax.shard_map(
        functools.partial(body, seq // 16, 16),
        mesh=fine,
        in_specs=in_specs,
        out_specs=P(("zh", "g", "mp"), None),
        check_vma=False,
    )
```

```python
import functools

import jax
import jax.numpy as jnp
from jax import lax
from jax.experimental import pallas as pl
from jax.experimental.pallas import tpu as pltpu
from jax.sharding import Mesh, PartitionSpec as P

HEAD_DIM = 128
F32 = jnp.float32
B16 = jnp.bfloat16
EXTRA = 8


def pieces3(a):
    hi = a.astype(B16)
    rest = a - hi.astype(F32)
    mid = rest.astype(B16)
    return hi, mid, (rest - mid.astype(F32)).astype(B16)


def triangle(n):
    r = lax.broadcasted_iota(jnp.int32, (n, n), 0)
    c = lax.broadcasted_iota(jnp.int32, (n, n), 1)
    return r >= c


def cumulative(gt, columns):
    low = triangle(gt.shape[1]).astype(F32).astype(B16)
    hi, mid, lo = (
        lax.dot_general(
            low if columns else p,
            p if columns else low,
            (((1,), (1,)), ((), ())),
            preferred_element_type=F32,
        )
        for p in pieces3(gt)
    )
    return hi + (mid + lo)


def decay_rows(d):
    d = jnp.broadcast_to(d, (EXTRA, HEAD_DIM))
    hi, mid, lo = (p.astype(F32) for p in pieces3(d))
    row = lax.broadcasted_iota(jnp.int32, d.shape, 0)
    out = jnp.where(row == 0, hi, jnp.where(row == 1, mid, jnp.where(row == 2, lo, 0.0)))
    return out.astype(B16)


def read_decay(rows):
    r = rows.astype(F32)
    return r[0:1] + (r[1:2] + r[2:3])


def states_kernel(k_hbm, v_hbm, g_hbm, o_hbm, k_ref, v_ref, g_ref, o_ref, sems, out_sems):
    heads = g_ref.shape[0]
    half = o_ref.shape[1] - EXTRA
    cuts = HEAD_DIM // half
    gates, *copies = [
        pltpu.make_async_copy(g_hbm, g_ref, sems.at[0]),
        pltpu.make_async_copy(k_hbm, k_ref, sems.at[1]),
        pltpu.make_async_copy(v_hbm, v_ref, sems.at[2]),
    ]
    for copy in (gates, *copies):
        copy.start()
    gates.wait()
    cum = cumulative(g_ref[...], True)
    last = cum[-1:]
    to_end = jnp.exp(last - cum)
    whole = jnp.exp(last)
    for copy in copies:
        copy.wait()
    leaving = []
    for h in range(heads):
        cols = slice(h * HEAD_DIM, (h + 1) * HEAD_DIM)
        scaled = (k_ref[:, cols].astype(F32) * to_end[:, h : h + 1]).astype(B16)
        state = lax.dot_general(
            scaled, v_ref[:, cols], (((0,), (0,)), ((), ())), preferred_element_type=F32
        ).astype(B16)
        rows = decay_rows(whole[:, h : h + 1])
        for i in range(cuts):
            o_ref[h * cuts + i, :half] = state[i * half : (i + 1) * half]
            o_ref[h * cuts + i, half:] = rows
        part = pl.ds(h * cuts, cuts)
        leaving.append(pltpu.make_async_copy(o_ref.at[part], o_hbm.at[part], out_sems.at[h]))
        leaving[-1].start()
    for copy in leaving:
        copy.wait()


def total_kernel(order, x_ref, *refs):
    *o_refs, d_ref = refs
    n, rows, _ = x_ref.shape
    half = rows - EXTRA
    for b in range(n):
        at = order.index(b)
        d = read_decay(x_ref[at, half:])
        d_ref[b : b + 1] = d
        s = x_ref[at, :half].astype(F32)
        state = d * state + s if b else s
        decay = decay * d if b else d
    state = state.astype(B16)
    tail = decay_rows(decay)
    for o_ref in o_refs:
        for j in range(o_ref.shape[0]):
            o_ref[j, :half] = state
            o_ref[j, half:] = tail


def sum_kernel(order, *refs):
    *first, z_ref, o_ref = refs
    half = o_ref.shape[0]
    state = first[0][...].astype(F32) if first else jnp.zeros((half, HEAD_DIM), F32)
    for j in range(z_ref.shape[0]):
        at = order.index(j)
        state = read_decay(z_ref[at, half:]) * state + z_ref[at, :half].astype(F32)
    o_ref[...] = state.astype(B16)


def prior_kernel(pair, four, order, place_ref, z0_ref, z1_ref, z2_ref, p1_ref, pa_ref, pb_ref, x_ref, d_ref, o_ref):
    n, half, _ = o_ref.shape
    zh = place_ref[0]
    second, late = zh >= 2, zh >= 4
    by_a = (zh == 5) | (zh == 6)
    place = jnp.where(late, zh - 4, jnp.where(second, zh - 2, zh))
    came = jnp.where(by_a, pa_ref[...].astype(F32), pb_ref[...].astype(F32))
    state = jnp.where(late, came, jnp.where(second, p1_ref[...].astype(F32), 0.0))
    for j in range(len(four) - 1):
        at = four.index(j)
        decay, own = read_decay(z2_ref[at, half:]), z2_ref[at, :half].astype(F32)
        if j == 0:
            at = pair.index(j)
            for ref, take in ((z1_ref, late), (z0_ref, second)):
                decay_e, own_e = read_decay(ref[at, half:]), ref[at, :half].astype(F32)
                decay, own = jnp.where(take, decay, decay_e), jnp.where(take, own, own_e)
        state = jnp.where(j < place, decay * state + own, state)
    for b in range(n):
        at = order.index(b)
        o_ref[at] = state.astype(B16)
        if b < n - 1:
            state = d_ref[b : b + 1] * state + x_ref[at, :half].astype(F32)


def inner_kernel(q_ref, k_ref, v_ref, g_ref, o_ref, e_ref):
    heads, tok = g_ref.shape
    cum = cumulative(g_ref[...], True)
    cum_t = cumulative(g_ref[...], False)
    e_ref[...] = jnp.exp(cum)
    causal = triangle(tok)
    for h in range(heads):
        cols = slice(h * HEAD_DIM, (h + 1) * HEAD_DIM)
        scores = lax.dot_general(
            q_ref[:, cols], k_ref[:, cols], (((1,), (1,)), ((), ())), preferred_element_type=F32
        )
        diff = cum[:, h : h + 1] - cum_t[h : h + 1, :]
        factor = jnp.where(causal, jnp.exp(jnp.minimum(diff, 0.0)), 0.0)
        weights = (scores * factor).astype(B16)
        o_ref[:, cols] = jnp.dot(weights, v_ref[:, cols], preferred_element_type=F32)


def output_kernel(order, q_ref, s_ref, i_ref, e_ref, gain_ref, o_ref):
    heads = e_ref.shape[1]
    grown = e_ref[...]
    for h in range(heads):
        cols = slice(h * HEAD_DIM, (h + 1) * HEAD_DIM)
        outer = jnp.dot(q_ref[:, cols], s_ref[h], preferred_element_type=F32)
        mixed = i_ref[:, cols] + outer * grown[:, h : h + 1]
        mean = jnp.mean(mixed * mixed, axis=-1, keepdims=True)
        normed = (mixed * lax.rsqrt(mean + 1e-05) * gain_ref[:, cols]).astype(B16)
        quarter = o_ref.shape[1]
        for j, place in enumerate(order):
            o_ref[j, :, cols] = normed[place * quarter : (place + 1) * quarter]


def local(kernel, outs, *args, flops=0, spaces=(), out=pltpu.VMEM, scratch=(), vmem=32):
    spaces = (*spaces, *(pltpu.VMEM,) * (len(args) - len(spaces)))
    moved = sum(a.size * a.dtype.itemsize for a in args)
    return pl.pallas_call(
        kernel,
        out_shape=[jax.ShapeDtypeStruct(shape, dtype) for shape, dtype in outs],
        in_specs=[pl.BlockSpec(memory_space=space) for space in spaces],
        out_specs=[pl.BlockSpec(memory_space=out)] * len(outs),
        scratch_shapes=scratch,
        compiler_params=pltpu.CompilerParams(vmem_limit_bytes=vmem * 2**20),
        cost_estimate=pl.CostEstimate(flops=flops, bytes_accessed=moved, transcendentals=0),
    )(*args)


def rotated(n, first):
    return [(first + j) % n for j in range(n)]


def exchange(a, axis, order):
    return lax.all_to_all(a, axis, 0, 0, tiled=True, axis_index_groups=[order])


def body(groups, members, queries, keys, values, log_decay, norm_gain):
    tok, width = queries.shape
    heads = log_decay.shape[1]
    mps = lax.axis_size("mp")
    half = heads * HEAD_DIM // members
    mac = 2 * heads * tok * HEAD_DIM * HEAD_DIM
    assert groups == 8
    pair, four = [1, 0], [1, 3, 2, 0]
    order = rotated(members, (13 * members) // 16)
    y_order = rotated(mps, mps // 2)
    gates = log_decay.T
    (own,) = local(
        states_kernel,
        [((members, half + EXTRA, HEAD_DIM), B16)],
        keys,
        values,
        gates,
        flops=mac,
        spaces=(pl.ANY,) * 3,
        out=pl.ANY,
        scratch=[
            pltpu.VMEM((tok, width), B16),
            pltpu.VMEM((tok, width), B16),
            pltpu.VMEM((heads, tok), F32),
            pltpu.VMEM((members, half + EXTRA, HEAD_DIM), B16),
            pltpu.SemaphoreType.DMA((3,)),
            pltpu.SemaphoreType.DMA((heads,)),
        ],
        vmem=60,
    )
    blocks = exchange(own, "g", order)
    inner, grown = local(
        inner_kernel,
        [((tok, width), F32), ((tok, heads), F32)],
        queries,
        keys,
        values,
        gates,
        flops=2 * mac,
    )
    blocks, inner, grown = lax.optimization_barrier((blocks, inner, grown))
    rows = half + EXTRA
    total2, total4, decays = local(
        functools.partial(total_kernel, order),
        [((2, rows, HEAD_DIM), B16), ((4, rows, HEAD_DIM), B16), ((members, HEAD_DIM), F32)],
        blocks,
    )
    zh = lax.axis_index("zh")
    place = zh.astype(jnp.int32).reshape(1)

    def among(group):
        n = len(group)
        lists = [[first + j for j in group] for first in range(0, groups, n)]
        return lambda a: lax.all_to_all(a, "zh", 0, 0, tiled=True, axis_index_groups=lists)

    def same(a):
        return a

    def added(*args):
        return local(functools.partial(sum_kernel, pair), [((half, HEAD_DIM), B16)], *args)[0]

    z0 = lax.cond(zh < 2, among(pair), same, total2)
    sum0 = added(z0)
    first = lax.ppermute(sum0, "zh", [(0, 2), (1, 3)])
    total2, sum0 = lax.optimization_barrier((total2, sum0))
    z1 = lax.cond((zh >= 2) & (zh < 4), among(pair), same, total2)
    sum1 = added(first, z1)
    came_a = lax.ppermute(sum1, "zh", [(3, 5), (2, 6)])
    came_b = lax.ppermute(sum1, "zh", [(3, 4), (2, 7)])
    total4, sum1 = lax.optimization_barrier((total4, sum1))
    z2 = lax.cond(zh >= 4, among(four), same, total4)
    (prior,) = local(
        functools.partial(prior_kernel, pair, four, order),
        [((members, half, HEAD_DIM), B16)],
        place,
        z0,
        z1,
        z2,
        first,
        came_a,
        came_b,
        blocks,
        decays,
        spaces=(pltpu.SMEM,),
    )
    state = exchange(prior, "g", order).reshape(heads, HEAD_DIM, HEAD_DIM)
    (normed,) = local(
        functools.partial(output_kernel, y_order),
        [((mps, tok // mps, width), B16)],
        queries,
        state,
        inner,
        grown,
        norm_gain.reshape(1, width),
        flops=mac,
    )
    arrived = exchange(normed, "mp", y_order)
    return jnp.concatenate([arrived[y_order.index(y)] for y in range(mps)], axis=1)


def solution(mesh):
    seq, mp = mesh.devices.shape
    fine = Mesh(mesh.devices.reshape(seq // 16, 16, mp), ("zh", "g", "mp"))
    in_specs = (P(("zh", "g"), "mp"),) * 4 + (P("mp"),)
    return jax.shard_map(
        functools.partial(body, seq // 16, 16),
        mesh=fine,
        in_specs=in_specs,
        out_specs=P(("zh", "g", "mp"), None),
        check_vma=False,
    )
```

```python
import functools

import jax
import jax.numpy as jnp
from jax import lax
from jax.experimental import pallas as pl
from jax.experimental.pallas import tpu as pltpu
from jax.sharding import Mesh, PartitionSpec as P

HEAD_DIM = 128
F32 = jnp.float32
B16 = jnp.bfloat16
EXTRA = 8


def pieces3(a):
    hi = a.astype(B16)
    rest = a - hi.astype(F32)
    mid = rest.astype(B16)
    return hi, mid, (rest - mid.astype(F32)).astype(B16)


def triangle(n):
    r = lax.broadcasted_iota(jnp.int32, (n, n), 0)
    c = lax.broadcasted_iota(jnp.int32, (n, n), 1)
    return r >= c


def cumulative(gt, columns):
    low = triangle(gt.shape[1]).astype(F32).astype(B16)
    hi, mid, lo = (
        lax.dot_general(
            low if columns else p,
            p if columns else low,
            (((1,), (1,)), ((), ())),
            preferred_element_type=F32,
        )
        for p in pieces3(gt)
    )
    return hi + (mid + lo)


def decay_rows(d):
    d = jnp.broadcast_to(d, (EXTRA, HEAD_DIM))
    hi, mid, lo = (p.astype(F32) for p in pieces3(d))
    row = lax.broadcasted_iota(jnp.int32, d.shape, 0)
    out = jnp.where(row == 0, hi, jnp.where(row == 1, mid, jnp.where(row == 2, lo, 0.0)))
    return out.astype(B16)


def read_decay(rows):
    r = rows.astype(F32)
    return r[0:1] + (r[1:2] + r[2:3])


def states_kernel(k_hbm, v_hbm, g_hbm, o_hbm, k_ref, v_ref, g_ref, o_ref, sems, out_sems):
    heads = g_ref.shape[0]
    half = o_ref.shape[1] - EXTRA
    cuts = HEAD_DIM // half
    gates, *copies = [
        pltpu.make_async_copy(g_hbm, g_ref, sems.at[0]),
        pltpu.make_async_copy(k_hbm, k_ref, sems.at[1]),
        pltpu.make_async_copy(v_hbm, v_ref, sems.at[2]),
    ]
    for copy in (gates, *copies):
        copy.start()
    gates.wait()
    cum = cumulative(g_ref[...], True)
    last = cum[-1:]
    to_end = jnp.exp(last - cum)
    whole = jnp.exp(last)
    for copy in copies:
        copy.wait()
    leaving = []
    for h in range(heads):
        cols = slice(h * HEAD_DIM, (h + 1) * HEAD_DIM)
        scaled = (k_ref[:, cols].astype(F32) * to_end[:, h : h + 1]).astype(B16)
        state = lax.dot_general(
            scaled, v_ref[:, cols], (((0,), (0,)), ((), ())), preferred_element_type=F32
        ).astype(B16)
        rows = decay_rows(whole[:, h : h + 1])
        for i in range(cuts):
            o_ref[h * cuts + i, :half] = state[i * half : (i + 1) * half]
            o_ref[h * cuts + i, half:] = rows
        part = pl.ds(h * cuts, cuts)
        leaving.append(pltpu.make_async_copy(o_ref.at[part], o_hbm.at[part], out_sems.at[h]))
        leaving[-1].start()
    for copy in leaving:
        copy.wait()


def total_kernel(order, x_ref, *refs):
    *o_refs, d_ref = refs
    n, rows, _ = x_ref.shape
    half = rows - EXTRA
    for b in range(n):
        at = order.index(b)
        d = read_decay(x_ref[at, half:])
        d_ref[b : b + 1] = d
        s = x_ref[at, :half].astype(F32)
        state = d * state + s if b else s
        decay = decay * d if b else d
    state = state.astype(B16)
    tail = decay_rows(decay)
    for o_ref in o_refs:
        for j in range(o_ref.shape[0]):
            o_ref[j, :half] = state
            o_ref[j, half:] = tail


def sum_kernel(order, *refs):
    *first, z_ref, o_ref = refs
    half = o_ref.shape[0]
    state = first[0][...].astype(F32) if first else jnp.zeros((half, HEAD_DIM), F32)
    for j in range(z_ref.shape[0]):
        at = order.index(j)
        state = read_decay(z_ref[at, half:]) * state + z_ref[at, :half].astype(F32)
    o_ref[...] = state.astype(B16)


def prior_kernel(pair, four, order, place_ref, z0_ref, z1_ref, z2_ref, p1_ref, pa_ref, pb_ref, x_ref, d_ref, o_ref):
    n, half, _ = o_ref.shape
    zh = place_ref[0]
    second, late = zh >= 2, zh >= 4
    by_a = (zh == 4) | (zh == 7)
    place = jnp.where(late, zh - 4, jnp.where(second, zh - 2, zh))
    came = jnp.where(by_a, pa_ref[...].astype(F32), pb_ref[...].astype(F32))
    state = jnp.where(late, came, jnp.where(second, p1_ref[...].astype(F32), 0.0))
    for j in range(len(four) - 1):
        at = four.index(j)
        decay, own = read_decay(z2_ref[at, half:]), z2_ref[at, :half].astype(F32)
        if j == 0:
            at = pair.index(j)
            for ref, take in ((z1_ref, late), (z0_ref, second)):
                decay_e, own_e = read_decay(ref[at, half:]), ref[at, :half].astype(F32)
                decay, own = jnp.where(take, decay, decay_e), jnp.where(take, own, own_e)
        state = jnp.where(j < place, decay * state + own, state)
    for b in range(n):
        at = order.index(b)
        o_ref[at] = state.astype(B16)
        if b < n - 1:
            state = d_ref[b : b + 1] * state + x_ref[at, :half].astype(F32)


def inner_kernel(q_ref, k_ref, v_ref, g_ref, o_ref, e_ref):
    heads, tok = g_ref.shape
    cum = cumulative(g_ref[...], True)
    cum_t = cumulative(g_ref[...], False)
    e_ref[...] = jnp.exp(cum)
    causal = triangle(tok)
    for h in range(heads):
        cols = slice(h * HEAD_DIM, (h + 1) * HEAD_DIM)
        scores = lax.dot_general(
            q_ref[:, cols], k_ref[:, cols], (((1,), (1,)), ((), ())), preferred_element_type=F32
        )
        diff = cum[:, h : h + 1] - cum_t[h : h + 1, :]
        factor = jnp.where(causal, jnp.exp(jnp.minimum(diff, 0.0)), 0.0)
        weights = (scores * factor).astype(B16)
        o_ref[:, cols] = jnp.dot(weights, v_ref[:, cols], preferred_element_type=F32)


def output_kernel(order, q_ref, s_ref, i_ref, e_ref, gain_ref, o_ref):
    heads = e_ref.shape[1]
    grown = e_ref[...]
    for h in range(heads):
        cols = slice(h * HEAD_DIM, (h + 1) * HEAD_DIM)
        outer = jnp.dot(q_ref[:, cols], s_ref[h], preferred_element_type=F32)
        mixed = i_ref[:, cols] + outer * grown[:, h : h + 1]
        mean = jnp.mean(mixed * mixed, axis=-1, keepdims=True)
        normed = (mixed * lax.rsqrt(mean + 1e-05) * gain_ref[:, cols]).astype(B16)
        quarter = o_ref.shape[1]
        for j, place in enumerate(order):
            o_ref[j, :, cols] = normed[place * quarter : (place + 1) * quarter]


def local(kernel, outs, *args, flops=0, spaces=(), out=pltpu.VMEM, scratch=(), vmem=32):
    spaces = (*spaces, *(pltpu.VMEM,) * (len(args) - len(spaces)))
    moved = sum(a.size * a.dtype.itemsize for a in args)
    return pl.pallas_call(
        kernel,
        out_shape=[jax.ShapeDtypeStruct(shape, dtype) for shape, dtype in outs],
        in_specs=[pl.BlockSpec(memory_space=space) for space in spaces],
        out_specs=[pl.BlockSpec(memory_space=out)] * len(outs),
        scratch_shapes=scratch,
        compiler_params=pltpu.CompilerParams(vmem_limit_bytes=vmem * 2**20),
        cost_estimate=pl.CostEstimate(flops=flops, bytes_accessed=moved, transcendentals=0),
    )(*args)


def rotated(n, first):
    return [(first + j) % n for j in range(n)]


def exchange(a, axis, order):
    return lax.all_to_all(a, axis, 0, 0, tiled=True, axis_index_groups=[order])


def body(groups, members, queries, keys, values, log_decay, norm_gain):
    tok, width = queries.shape
    heads = log_decay.shape[1]
    mps = lax.axis_size("mp")
    half = heads * HEAD_DIM // members
    mac = 2 * heads * tok * HEAD_DIM * HEAD_DIM
    assert groups == 8
    pair, four = [1, 0], [1, 3, 2, 0]
    order = rotated(members, (13 * members) // 16)
    y_order = rotated(mps, mps // 2)
    gates = log_decay.T
    (own,) = local(
        states_kernel,
        [((members, half + EXTRA, HEAD_DIM), B16)],
        keys,
        values,
        gates,
        flops=mac,
        spaces=(pl.ANY,) * 3,
        out=pl.ANY,
        scratch=[
            pltpu.VMEM((tok, width), B16),
            pltpu.VMEM((tok, width), B16),
            pltpu.VMEM((heads, tok), F32),
            pltpu.VMEM((members, half + EXTRA, HEAD_DIM), B16),
            pltpu.SemaphoreType.DMA((3,)),
            pltpu.SemaphoreType.DMA((heads,)),
        ],
        vmem=60,
    )
    blocks = exchange(own, "g", order)
    inner, grown = local(
        inner_kernel,
        [((tok, width), F32), ((tok, heads), F32)],
        queries,
        keys,
        values,
        gates,
        flops=2 * mac,
    )
    blocks, inner, grown = lax.optimization_barrier((blocks, inner, grown))
    rows = half + EXTRA
    total2, total4, decays = local(
        functools.partial(total_kernel, order),
        [((2, rows, HEAD_DIM), B16), ((4, rows, HEAD_DIM), B16), ((members, HEAD_DIM), F32)],
        blocks,
    )
    zh = lax.axis_index("zh")
    place = zh.astype(jnp.int32).reshape(1)

    def among(group):
        n = len(group)
        lists = [[first + j for j in group] for first in range(0, groups, n)]
        return lambda a: lax.all_to_all(a, "zh", 0, 0, tiled=True, axis_index_groups=lists)

    def same(a):
        return a

    def added(*args):
        return local(functools.partial(sum_kernel, pair), [((half, HEAD_DIM), B16)], *args)[0]

    z0 = lax.cond(zh < 2, among(pair), same, total2)
    sum0 = added(z0)
    first = lax.ppermute(sum0, "zh", [(0, 2), (1, 3)])
    total2, sum0 = lax.optimization_barrier((total2, sum0))
    z1 = lax.cond((zh >= 2) & (zh < 4), among(pair), same, total2)
    sum1 = added(first, z1)
    came_a = lax.ppermute(sum1, "zh", [(3, 4), (2, 7)])
    came_b = lax.ppermute(sum1, "zh", [(3, 6), (2, 5)])
    total4, sum1 = lax.optimization_barrier((total4, sum1))
    z2 = lax.cond(zh >= 4, among(four), same, total4)
    (prior,) = local(
        functools.partial(prior_kernel, pair, four, order),
        [((members, half, HEAD_DIM), B16)],
        place,
        z0,
        z1,
        z2,
        first,
        came_a,
        came_b,
        blocks,
        decays,
        spaces=(pltpu.SMEM,),
    )
    state = exchange(prior, "g", order).reshape(heads, HEAD_DIM, HEAD_DIM)
    (normed,) = local(
        functools.partial(output_kernel, y_order),
        [((mps, tok // mps, width), B16)],
        queries,
        state,
        inner,
        grown,
        norm_gain.reshape(1, width),
        flops=mac,
    )
    arrived = exchange(normed, "mp", y_order)
    return jnp.concatenate([arrived[y_order.index(y)] for y in range(mps)], axis=1)


def solution(mesh):
    seq, mp = mesh.devices.shape
    fine = Mesh(mesh.devices.reshape(seq // 16, 16, mp), ("zh", "g", "mp"))
    in_specs = (P(("zh", "g"), "mp"),) * 4 + (P("mp"),)
    return jax.shard_map(
        functools.partial(body, seq // 16, 16),
        mesh=fine,
        in_specs=in_specs,
        out_specs=P(("zh", "g", "mp"), None),
        check_vma=False,
    )
```

```python
import functools

import jax
import jax.numpy as jnp
from jax import lax
from jax.experimental import pallas as pl
from jax.experimental.pallas import tpu as pltpu
from jax.sharding import Mesh, PartitionSpec as P

HEAD_DIM = 128
F32 = jnp.float32
B16 = jnp.bfloat16
EXTRA = 8


def pieces3(a):
    hi = a.astype(B16)
    rest = a - hi.astype(F32)
    mid = rest.astype(B16)
    return hi, mid, (rest - mid.astype(F32)).astype(B16)


def triangle(n):
    r = lax.broadcasted_iota(jnp.int32, (n, n), 0)
    c = lax.broadcasted_iota(jnp.int32, (n, n), 1)
    return r >= c


def cumulative(gt, columns):
    low = triangle(gt.shape[1]).astype(F32).astype(B16)
    hi, mid, lo = (
        lax.dot_general(
            low if columns else p,
            p if columns else low,
            (((1,), (1,)), ((), ())),
            preferred_element_type=F32,
        )
        for p in pieces3(gt)
    )
    return hi + (mid + lo)


def decay_rows(d):
    d = jnp.broadcast_to(d, (EXTRA, HEAD_DIM))
    hi, mid, lo = (p.astype(F32) for p in pieces3(d))
    row = lax.broadcasted_iota(jnp.int32, d.shape, 0)
    out = jnp.where(row == 0, hi, jnp.where(row == 1, mid, jnp.where(row == 2, lo, 0.0)))
    return out.astype(B16)


def read_decay(rows):
    r = rows.astype(F32)
    return r[0:1] + (r[1:2] + r[2:3])


def states_kernel(k_hbm, v_hbm, g_hbm, o_hbm, k_ref, v_ref, g_ref, o_ref, sems, out_sems):
    heads = g_ref.shape[0]
    half = o_ref.shape[1] - EXTRA
    cuts = HEAD_DIM // half
    gates, *copies = [
        pltpu.make_async_copy(g_hbm, g_ref, sems.at[0]),
        pltpu.make_async_copy(k_hbm, k_ref, sems.at[1]),
        pltpu.make_async_copy(v_hbm, v_ref, sems.at[2]),
    ]
    for copy in (gates, *copies):
        copy.start()
    gates.wait()
    cum = cumulative(g_ref[...], True)
    last = cum[-1:]
    to_end = jnp.exp(last - cum)
    whole = jnp.exp(last)
    for copy in copies:
        copy.wait()
    leaving = []
    for h in range(heads):
        cols = slice(h * HEAD_DIM, (h + 1) * HEAD_DIM)
        scaled = (k_ref[:, cols].astype(F32) * to_end[:, h : h + 1]).astype(B16)
        state = lax.dot_general(
            scaled, v_ref[:, cols], (((0,), (0,)), ((), ())), preferred_element_type=F32
        ).astype(B16)
        rows = decay_rows(whole[:, h : h + 1])
        for i in range(cuts):
            o_ref[h * cuts + i, :half] = state[i * half : (i + 1) * half]
            o_ref[h * cuts + i, half:] = rows
        part = pl.ds(h * cuts, cuts)
        leaving.append(pltpu.make_async_copy(o_ref.at[part], o_hbm.at[part], out_sems.at[h]))
        leaving[-1].start()
    for copy in leaving:
        copy.wait()


def total_kernel(order, x_ref, *refs):
    *o_refs, d_ref = refs
    n, rows, _ = x_ref.shape
    half = rows - EXTRA
    for b in range(n):
        at = order.index(b)
        d = read_decay(x_ref[at, half:])
        d_ref[b : b + 1] = d
        s = x_ref[at, :half].astype(F32)
        state = d * state + s if b else s
        decay = decay * d if b else d
    state = state.astype(B16)
    tail = decay_rows(decay)
    for o_ref in o_refs:
        for j in range(o_ref.shape[0]):
            o_ref[j, :half] = state
            o_ref[j, half:] = tail


def sum_kernel(order, *refs):
    *first, z_ref, o_ref = refs
    half = o_ref.shape[0]
    state = first[0][...].astype(F32) if first else jnp.zeros((half, HEAD_DIM), F32)
    for j in range(z_ref.shape[0]):
        at = order.index(j)
        state = read_decay(z_ref[at, half:]) * state + z_ref[at, :half].astype(F32)
    o_ref[...] = state.astype(B16)


def prior_kernel(pair, four, order, place_ref, z0_ref, z1_ref, z2_ref, p1_ref, pa_ref, pb_ref, x_ref, d_ref, o_ref):
    n, half, _ = o_ref.shape
    zh = place_ref[0]
    second, late = zh >= 2, zh >= 4
    by_a = (zh == 4) | (zh == 7)
    place = jnp.where(late, zh - 4, jnp.where(second, zh - 2, zh))
    came = jnp.where(by_a, pa_ref[...].astype(F32), pb_ref[...].astype(F32))
    state = jnp.where(late, came, jnp.where(second, p1_ref[...].astype(F32), 0.0))
    for j in range(len(four) - 1):
        at = four.index(j)
        decay, own = read_decay(z2_ref[at, half:]), z2_ref[at, :half].astype(F32)
        if j == 0:
            at = pair.index(j)
            for ref, take in ((z1_ref, late), (z0_ref, second)):
                decay_e, own_e = read_decay(ref[at, half:]), ref[at, :half].astype(F32)
                decay, own = jnp.where(take, decay, decay_e), jnp.where(take, own, own_e)
        state = jnp.where(j < place, decay * state + own, state)
    for b in range(n):
        at = order.index(b)
        o_ref[at] = state.astype(B16)
        if b < n - 1:
            state = d_ref[b : b + 1] * state + x_ref[at, :half].astype(F32)


def inner_kernel(q_ref, k_ref, v_ref, g_ref, o_ref, e_ref):
    heads, tok = g_ref.shape
    cum = cumulative(g_ref[...], True)
    cum_t = cumulative(g_ref[...], False)
    e_ref[...] = jnp.exp(cum)
    causal = triangle(tok)
    for h in range(heads):
        cols = slice(h * HEAD_DIM, (h + 1) * HEAD_DIM)
        scores = lax.dot_general(
            q_ref[:, cols], k_ref[:, cols], (((1,), (1,)), ((), ())), preferred_element_type=F32
        )
        diff = cum[:, h : h + 1] - cum_t[h : h + 1, :]
        factor = jnp.where(causal, jnp.exp(jnp.minimum(diff, 0.0)), 0.0)
        weights = (scores * factor).astype(B16)
        o_ref[:, cols] = jnp.dot(weights, v_ref[:, cols], preferred_element_type=F32)


def output_kernel(order, q_ref, s_ref, i_ref, e_ref, gain_ref, o_ref):
    heads = e_ref.shape[1]
    grown = e_ref[...]
    for h in range(heads):
        cols = slice(h * HEAD_DIM, (h + 1) * HEAD_DIM)
        outer = jnp.dot(q_ref[:, cols], s_ref[h], preferred_element_type=F32)
        mixed = i_ref[:, cols] + outer * grown[:, h : h + 1]
        mean = jnp.mean(mixed * mixed, axis=-1, keepdims=True)
        normed = (mixed * lax.rsqrt(mean + 1e-05) * gain_ref[:, cols]).astype(B16)
        quarter = o_ref.shape[1]
        for j, place in enumerate(order):
            o_ref[j, :, cols] = normed[place * quarter : (place + 1) * quarter]


def local(kernel, outs, *args, flops=0, spaces=(), out=pltpu.VMEM, scratch=(), vmem=32):
    spaces = (*spaces, *(pltpu.VMEM,) * (len(args) - len(spaces)))
    moved = sum(a.size * a.dtype.itemsize for a in args)
    return pl.pallas_call(
        kernel,
        out_shape=[jax.ShapeDtypeStruct(shape, dtype) for shape, dtype in outs],
        in_specs=[pl.BlockSpec(memory_space=space) for space in spaces],
        out_specs=[pl.BlockSpec(memory_space=out)] * len(outs),
        scratch_shapes=scratch,
        compiler_params=pltpu.CompilerParams(vmem_limit_bytes=vmem * 2**20),
        cost_estimate=pl.CostEstimate(flops=flops, bytes_accessed=moved, transcendentals=0),
    )(*args)


def rotated(n, first):
    return [(first + j) % n for j in range(n)]


def exchange(a, axis, order):
    return lax.all_to_all(a, axis, 0, 0, tiled=True, axis_index_groups=[order])


def body(groups, members, queries, keys, values, log_decay, norm_gain):
    tok, width = queries.shape
    heads = log_decay.shape[1]
    mps = lax.axis_size("mp")
    half = heads * HEAD_DIM // members
    mac = 2 * heads * tok * HEAD_DIM * HEAD_DIM
    assert groups == 8
    pair, four = [1, 0], [1, 0, 3, 2]
    order = rotated(members, (5 * members) // 16)
    y_order = [mps // 2, *(y for y in range(mps) if y != mps // 2)]
    gates = log_decay.T
    (own,) = local(
        states_kernel,
        [((members, half + EXTRA, HEAD_DIM), B16)],
        keys,
        values,
        gates,
        flops=mac,
        spaces=(pl.ANY,) * 3,
        out=pl.ANY,
        scratch=[
            pltpu.VMEM((tok, width), B16),
            pltpu.VMEM((tok, width), B16),
            pltpu.VMEM((heads, tok), F32),
            pltpu.VMEM((members, half + EXTRA, HEAD_DIM), B16),
            pltpu.SemaphoreType.DMA((3,)),
            pltpu.SemaphoreType.DMA((heads,)),
        ],
        vmem=60,
    )
    blocks = exchange(own, "g", order)
    inner, grown = local(
        inner_kernel,
        [((tok, width), F32), ((tok, heads), F32)],
        queries,
        keys,
        values,
        gates,
        flops=2 * mac,
    )
    blocks, inner, grown = lax.optimization_barrier((blocks, inner, grown))
    rows = half + EXTRA
    total2, total4, decays = local(
        functools.partial(total_kernel, order),
        [((2, rows, HEAD_DIM), B16), ((4, rows, HEAD_DIM), B16), ((members, HEAD_DIM), F32)],
        blocks,
    )
    zh = lax.axis_index("zh")
    place = zh.astype(jnp.int32).reshape(1)

    def among(group):
        n = len(group)
        lists = [[first + j for j in group] for first in range(0, groups, n)]
        return lambda a: lax.all_to_all(a, "zh", 0, 0, tiled=True, axis_index_groups=lists)

    def same(a):
        return a

    def added(*args):
        return local(functools.partial(sum_kernel, pair), [((half, HEAD_DIM), B16)], *args)[0]

    z0 = lax.cond(zh < 2, among(pair), same, total2)
    sum0 = added(z0)
    first = lax.ppermute(sum0, "zh", [(0, 2), (1, 3)])
    total2, sum0 = lax.optimization_barrier((total2, sum0))
    z1 = lax.cond((zh >= 2) & (zh < 4), among(pair), same, total2)
    sum1 = added(first, z1)
    came_a = lax.ppermute(sum1, "zh", [(3, 4), (2, 7)])
    came_b = lax.ppermute(sum1, "zh", [(3, 6), (2, 5)])
    total4, sum1 = lax.optimization_barrier((total4, sum1))
    z2 = lax.cond(zh >= 4, among(four), same, total4)
    (prior,) = local(
        functools.partial(prior_kernel, pair, four, order),
        [((members, half, HEAD_DIM), B16)],
        place,
        z0,
        z1,
        z2,
        first,
        came_a,
        came_b,
        blocks,
        decays,
        spaces=(pltpu.SMEM,),
    )
    state = exchange(prior, "g", order).reshape(heads, HEAD_DIM, HEAD_DIM)
    (normed,) = local(
        functools.partial(output_kernel, y_order),
        [((mps, tok // mps, width), B16)],
        queries,
        state,
        inner,
        grown,
        norm_gain.reshape(1, width),
        flops=mac,
    )
    arrived = exchange(normed, "mp", y_order)
    return jnp.concatenate([arrived[y_order.index(y)] for y in range(mps)], axis=1)


def solution(mesh):
    seq, mp = mesh.devices.shape
    fine = Mesh(mesh.devices.reshape(seq // 16, 16, mp), ("zh", "g", "mp"))
    in_specs = (P(("zh", "g"), "mp"),) * 4 + (P("mp"),)
    return jax.shard_map(
        functools.partial(body, seq // 16, 16),
        mesh=fine,
        in_specs=in_specs,
        out_specs=P(("zh", "g", "mp"), None),
        check_vma=False,
    )
```
